32 devices in a mesh: row: 4 (over x, core), col: 8 (over z, y).
Axes of the slice: x: 2, y: 2, z: 4, core: 2. Of those that a mesh axis runs over, the one named last changes fastest.
Arguments:
- front_matrix: float32 [16384, 16384], P('row', 'col'), may hold values from -2.5 to 202.5, as said below
- child_schur: float32 [2, 8192, 8192], P(None, 'row', 'col'), may hold values from -1.25 to 1.25
- child_index: int32 [2, 128], replicated, may hold values from 0 to 255, as said below
- child_valid: int32 [2, 128], replicated, may hold values 0 or 1
Outputs:
- trailing: float32 [16384, 16384], P('row', 'col')
- panel_factor: float32 [16384, 512], P('row')
The draws below stay inside these ranges and needn't reach their ends.
Inputs may be any that keep to these rules, and one draw needn't show every extreme that they name: `front_matrix`: off the logical diagonal the entries lie in -2.5 to 2.5, on it in 97.5 to 202.5. `child_index`: each child's 128 entries are distinct front blocks. Among the child blocks a that share a mod 4, exactly 8 land in front blocks of each value mod 4; among the child blocks b that share b mod 8, at most 2 land in front blocks of any one value mod 8, and some value takes exactly 2.
All inputs are finite; a program needn't handle non-finite values.
Results may differ from the reference program's by a relative error of at most 0.00005.
Values sent between devices are 32-bit elements; how exact they have to be, the bound alone decides.
A program may use at most 512 MiB of HBM per device.

```python
import jax
import jax.numpy as jnp
from jax import lax

FRONT = 16384
CHILD = 8192
PANEL = 512
BLK = 64
NB = 256
CB = 128
RB = 64
KB = 32
CC = 16
N_ROW = 4
N_COL = 8


def draw_front_matrix(key, part):
    row_devices = NB // RB
    col_devices = NB // KB
    base_key, diag_key = jax.random.split(key)
    entries = jax.random.truncated_normal(base_key, -2.5, 2.5, (FRONT, FRONT), jnp.float32)
    positions = jnp.arange(FRONT)
    stored_block = positions // BLK
    logical_row = (stored_block % RB * row_devices + stored_block // RB) * BLK + positions % BLK
    logical_col = (stored_block % KB * col_devices + stored_block // KB) * BLK + positions % BLK
    boost = jax.random.uniform(diag_key, (FRONT,), jnp.float32, 100.0, 200.0)
    return entries + jnp.where(logical_row[:, None] == logical_col[None, :], boost[logical_row][:, None], 0.0)


def draw_child_schur(key, part):
    return 0.5 * jax.random.truncated_normal(key, -2.5, 2.5, (2, CHILD, CHILD), jnp.float32)


def draw_child_index(key, part):
    col_devices = NB // KB
    lists = []
    for child_number in range(2):
        base = jax.random.fold_in(key, 17 + child_number)
        perm_key, shift_key, slot_key = jax.random.split(base, 3)
        orders = jax.vmap(lambda sub_key: jax.random.permutation(sub_key, CC))(jax.random.split(perm_key, col_devices))
        rotation = jax.random.randint(shift_key, (), 0, col_devices)
        all_blocks = jnp.arange(CB)
        column_group = all_blocks % col_devices
        column_step = all_blocks // col_devices
        residue = (column_group + orders[column_group, column_step] + rotation) % col_devices
        earlier = (residue[:, None] == residue[None, :]) & (all_blocks[None, :] < all_blocks[:, None])
        order_rank = jnp.sum(earlier.astype(jnp.int32), axis=1)
        slots = jax.vmap(lambda sub_key: jax.random.permutation(sub_key, KB))(jax.random.split(slot_key, col_devices))
        quotient = slots[residue, order_rank]
        lists.append(quotient * col_devices + residue)
    return jnp.stack(lists).astype(jnp.int32)


def touch_ends(result, rng, least, high):
    longest = result.shape.index(max(result.shape))
    spots = []
    for shift in (0, 1):
        where = [jax.random.randint(jax.random.fold_in(rng, axis), (), 0, length) for axis, length in enumerate(result.shape)]
        where[longest] = (where[longest] + shift) % result.shape[longest]
        spots.append(tuple(where))
    return result.at[spots[0]].set(least).at[spots[1]].set(high)


def setup_inputs(seed: int = 0) -> dict:
    keys = jax.random.split(jax.random.key(seed), 5)
    front_matrix = draw_front_matrix(jax.random.fold_in(keys[4], 71), 0)
    child_schur = draw_child_schur(jax.random.fold_in(keys[4], 71), 0)
    child_index = draw_child_index(jax.random.fold_in(keys[4], 71), 0)
    child_valid = touch_ends((jax.random.randint(keys[3], (2, CB), 0, 4) < 3).astype(jnp.int32), jax.random.fold_in(keys[3], 1), 0, 1)
    return dict(front_matrix=front_matrix, child_schur=child_schur, child_index=child_index, child_valid=child_valid)


def stored_rows(total_blocks, devices):
    per_device = total_blocks // devices
    logical = jnp.arange(total_blocks)
    stored = logical % devices * per_device + logical // devices
    return (stored[:, None] * BLK + jnp.arange(BLK)[None, :]).reshape(-1).astype(jnp.int32)

def reference(front_matrix, child_schur, child_index, child_valid):
    row_perm = stored_rows(NB, N_ROW)
    col_perm = stored_rows(NB, N_COL)
    front_l = front_matrix[row_perm][:, col_perm]
    blocked = front_l.reshape(NB, BLK, NB, BLK).transpose(0, 2, 1, 3)
    child_rows = stored_rows(CB, N_ROW)
    child_cols = stored_rows(CB, N_COL)
    for child_number in range(2):
        child_l = child_schur[child_number][child_rows][:, child_cols]
        pieces = child_l.reshape(CB, BLK, CB, BLK).transpose(0, 2, 1, 3)
        weight = child_valid[child_number].astype(jnp.float32)
        pieces = pieces * (weight[:, None] * weight[None, :])[:, :, None, None]
        target = child_index[child_number].astype(jnp.int32)
        blocked = blocked.at[target[:, None], target[None, :]].add(pieces)
    extended = blocked.transpose(0, 2, 1, 3).reshape(FRONT, FRONT)
    lower_factor = jnp.linalg.cholesky(extended[:PANEL, :PANEL])
    solved = jax.scipy.linalg.solve_triangular(lower_factor, extended[PANEL:, :PANEL].T, lower=True).T
    panel_l = jnp.concatenate([lower_factor, solved], axis=0)
    update = jnp.dot(panel_l.astype(jnp.float32), panel_l.T.astype(jnp.float32), precision=lax.Precision.HIGHEST, preferred_element_type=jnp.float32)
    retained = jnp.arange(FRONT) >= PANEL
    trailing_l = jnp.where(retained[:, None] & retained[None, :], extended - update, jnp.zeros_like(update))
    trailing = jnp.zeros_like(trailing_l).at[row_perm].set(trailing_l)
    trailing = jnp.zeros_like(trailing).at[:, col_perm].set(trailing)
    panel_factor = jnp.zeros((FRONT, PANEL), jnp.float32).at[row_perm].set(panel_l)
    return (trailing, panel_factor)
```

```python
import jax
import jax.numpy as jnp
from jax import lax
from jax.sharding import PartitionSpec as P

CHILD = 8192
PANEL = 512
BLK = 64


exact_mode = lax.Precision.HIGHEST
split_mode = lax.Precision.HIGH


def spread_2(shard, axis, root):
    mine = lax.axis_index(axis) == root
    return lax.psum(jnp.where(mine, shard, jnp.zeros_like(shard)), axis)


def on_device(front_matrix, child_schur, child_index, child_valid):
    row_count = lax.axis_size("row")
    col_count = lax.axis_size("col")
    row_place = lax.axis_index("row")
    col_place = lax.axis_index("col")
    local_rows, local_cols = front_matrix.shape
    row_blocks = local_rows // BLK
    col_blocks = local_cols // BLK
    child_blocks = CHILD // BLK
    child_rowblk = child_schur.shape[1] // BLK
    child_colblk = child_schur.shape[2] // BLK
    per_owner = child_blocks // (row_count * row_count)
    col_multi = max(1, child_blocks // (col_count * col_count))
    row_slots = row_count * per_owner
    col_slots = col_count * col_multi
    validity = child_valid.astype(jnp.float32)
    all_blocks = jnp.arange(child_blocks)
    owner_row = child_index % row_count
    owner_col = child_index % col_count
    sender_row = all_blocks % row_count
    sender_col = all_blocks % col_count
    before = all_blocks[None, :] < all_blocks[:, None]
    earlier_row = (sender_row[:, None] == sender_row[None, :]) & before
    earlier_col = (sender_col[:, None] == sender_col[None, :]) & before
    row_rank = jnp.sum(
        (earlier_row[None] & (owner_row[:, :, None] == owner_row[:, None, :])).astype(jnp.int32),
        axis=2,
    )
    col_rank = jnp.sum(
        (earlier_col[None] & (owner_col[:, :, None] == owner_col[:, None, :])).astype(jnp.int32),
        axis=2,
    )
    row_key = owner_row * per_owner + row_rank
    col_key = owner_col * col_multi + col_rank
    local_arow = row_place + row_count * jnp.arange(child_rowblk)
    mine_rowkey = jnp.take(row_key, local_arow, axis=1)
    row_hit_send = mine_rowkey[:, :, None] == jnp.arange(row_slots)[None, None, :]
    src_row = jnp.sum(
        row_hit_send.astype(jnp.int32) * jnp.arange(child_rowblk)[None, :, None], axis=1
    )
    local_bcol = col_place + col_count * jnp.arange(child_colblk)
    mine_colkey = jnp.take(col_key, local_bcol, axis=1)
    col_hit_send = mine_colkey[:, :, None] == jnp.arange(col_slots)[None, None, :]
    eye = jnp.eye(BLK, dtype=jnp.float32)
    chunk = col_multi * BLK
    sorter = col_hit_send.astype(jnp.float32)[:, :, None, :, None] * eye[None, None, :, None, :]
    sorter = sorter.reshape(2, child_colblk * BLK, col_slots * BLK)
    blocks = child_schur.reshape(2, child_rowblk, BLK, child_colblk * BLK)
    arrived = []
    for child in range(2):
        outgoing = jnp.take(blocks[child], src_row[child], axis=0, mode="clip")
        section_one = lax.all_to_all(outgoing, "row", split_axis=0, concat_axis=0, tiled=True)
        onward = jnp.dot(
            section_one.reshape(row_slots * BLK, child_colblk * BLK), sorter[child], precision=split_mode
        )
        onward = onward.reshape(row_slots * BLK, col_count, chunk).transpose(1, 0, 2)
        section_two = lax.all_to_all(onward, "col", split_axis=0, concat_axis=0, tiled=True)
        arrived.append(section_two.transpose(1, 0, 2).reshape(row_slots * BLK, col_slots * BLK))
    front_rowblk = row_place + row_count * jnp.arange(row_blocks)
    match_rows = (child_index[:, None, :] == front_rowblk[None, :, None]).astype(jnp.int32)
    row_slot_of = sender_row[None, :] * per_owner + row_rank
    row_source = jnp.sum(match_rows * row_slot_of[:, None, :], axis=2)
    row_weight = jnp.sum(match_rows.astype(jnp.float32) * validity[:, None, :], axis=2)
    front_colblk = col_place + col_count * jnp.arange(col_blocks)
    match_cols = (child_index[:, None, :] == front_colblk[None, :, None]).astype(jnp.int32)
    col_slot_of = sender_col[None, :] * col_multi + col_rank
    slot_hit = (col_slot_of[:, :, None] == jnp.arange(col_slots)[None, None, :]).astype(jnp.float32)
    placer = jnp.einsum(
        "kbs,kjb->ksj", slot_hit, match_cols.astype(jnp.float32) * validity[:, None, :], precision=exact_mode
    )
    placer = placer[:, :, None, :, None] * eye[None, None, :, None, :]
    placer = placer.reshape(2, col_slots * BLK, local_cols)
    extended = front_matrix.reshape(row_blocks, BLK, local_cols)
    for child in range(2):
        spread_cols = jnp.dot(arrived[child], placer[child], precision=split_mode)
        spread_cols = spread_cols.reshape(row_slots, BLK, local_cols)
        placed = jnp.take(spread_cols, row_source[child], axis=0, mode="clip")
        extended = extended + placed * row_weight[child][:, None, None]
    extended = extended.reshape(local_rows, local_cols)
    panel_width = PANEL // BLK
    half = local_rows // 2
    first = jnp.concatenate([extended[:half, :BLK], extended[half:, :BLK]], axis=1)
    gathered = lax.all_gather(first, "col")[:panel_width]
    panel_cols = gathered.reshape(panel_width, half, 2, BLK).transpose(2, 1, 0, 3)
    panel_cols = panel_cols.reshape(local_rows, PANEL)
    corner_count = panel_width // row_count
    corner_rows = lax.all_gather(panel_cols[: corner_count * BLK], "row")
    corner = corner_rows.reshape(row_count, corner_count, BLK, PANEL).transpose(1, 0, 2, 3)
    corner = corner.reshape(PANEL, PANEL)
    lower_factor = jnp.linalg.cholesky(corner)
    solved = jax.scipy.linalg.solve_triangular(lower_factor, panel_cols.T, lower=True).T
    logical_blk = jnp.arange(row_blocks) * row_count + row_place
    factor_blocks = lower_factor.reshape(panel_width, BLK, PANEL)
    picked = jnp.take(factor_blocks, jnp.minimum(logical_blk, panel_width - 1), axis=0)
    in_panel = (logical_blk < panel_width)[:, None, None]
    panel_factor = jnp.where(in_panel, picked, solved.reshape(row_blocks, BLK, PANEL)).reshape(
        local_rows, PANEL
    )
    spread = col_count // row_count
    arranged = panel_factor.reshape(col_blocks, spread, BLK, PANEL)
    chosen = lax.dynamic_index_in_dim(arranged, col_place // row_count, axis=1, keepdims=False)
    chosen = chosen.reshape(col_blocks * BLK, PANEL)
    across = spread_2(chosen, "row", col_place % row_count)
    update = jnp.einsum("rp,cp->rc", panel_factor, across, precision=split_mode)
    logical_row = jnp.arange(local_rows) // BLK * row_count + row_place
    logical_col = jnp.arange(local_cols) // BLK * col_count + col_place
    retained = (logical_row >= panel_width)[:, None] & (logical_col >= panel_width)[None, :]
    trailing = jnp.where(retained, extended - update, jnp.zeros_like(update))
    return (trailing, panel_factor)


def solution(mesh):
    in_specs = (P("row", "col"), P(None, "row", "col"), P(), P())
    out_specs = (P("row", "col"), P("row", None))
    return jax.shard_map(
        on_device, mesh=mesh, in_specs=in_specs, out_specs=out_specs, check_vma=False
    )
```
